256 devices in a mesh: seq: 16 (over y, x), filt: 8 (over z), dp: 2 (over core).
Axes of the slice: x: 4, y: 4, z: 8, core: 2. Of those that a mesh axis runs over, the one named last changes fastest.
Arguments:
- inputs: bfloat16 [2, 4096, 2048], P('dp', 'seq'), may hold values from -6 to 6
- filters: float32 [4096, 16], P(None, 'filt'), may hold values from -0.09375 to 0.09375
- weights: bfloat16 [16, 2048, 1024], P('filt'), may hold values from -0.03125 to 0.03125
- cotangent: bfloat16 [2, 4096, 1024], P('dp', ('seq', 'filt')), may hold values from -0.0625 to 0.0625
Outputs:
- outputs: bfloat16 [2, 4096, 1024], P('dp', ('seq', 'filt'))
- weight_grad: bfloat16 [2048, 16, 1024], P(('seq', 'dp'), 'filt')
The draws below stay inside these ranges and needn't reach their ends.
All inputs are finite; a program needn't handle non-finite values.
Results may differ from the reference program's by a relative error of at most 0.024.
Values may be sent and summed in bfloat16 or wider, within the bound.
No kernel may reach another device: no remote copies, remote signals or barrier semaphores. Data moves between devices by JAX's collectives and lax.ppermute only.
A program may use at most 128 MiB of HBM per device.

```python
import jax
import jax.numpy as jnp
from jax import lax

D = 2048
DO = 1024
K = 16
CH = 256
SEQS = 2
L = 4096
N_SEQ = 16


def with_spikes(drawn, key, source, target, blocks, factor):
    def block_of(position):
        return (jnp.arange(drawn.shape[position]) // (drawn.shape[position] // blocks)).reshape((-1,) + (1,) * (drawn.ndim - 1 - position))

    near = jax.random.permutation(key, blocks)[block_of(target)]
    other_side = (block_of(target) + blocks // 2) % blocks
    return jnp.where((block_of(source) == near) | (block_of(source) == other_side), factor * drawn, drawn)


def levels(key, shape, shards, low, high):
    gain, own = 1.0, jax.random.fold_in(key, 6)
    for axis_at, blocks in shards:
        steps = jnp.exp(jax.random.uniform(jax.random.fold_in(own, axis_at), (blocks,), jnp.float32, low / len(shards), high / len(shards)))
        gain = gain * jnp.repeat(steps, shape[axis_at] // blocks).reshape([-1 if axis == axis_at else 1 for axis in range(len(shape))])
    return gain


def centred(rng, dims, deviation, reach, split=(), kind=jnp.bfloat16):
    factor_of = levels(rng, dims, split, -0.22, 0.18) if split else 1.0
    result = jax.random.normal(rng, dims, jnp.float32) * deviation * factor_of
    return jnp.minimum(jnp.maximum(result, -reach), reach).astype(kind)


def gaussian_with(key, dims, width, reach, pieces, heavy, kind=jnp.bfloat16):
    entries = width * jax.random.normal(key, dims, jnp.float32)
    if pieces:
        entries = entries * levels(key, dims, pieces, -0.22, 0.18)
    return jnp.clip(with_spikes(entries, jax.random.fold_in(key, 3), *heavy), -reach, reach).astype(kind)


def setup_inputs(seed: int = 0) -> dict:
    key_of = jax.random.split(jax.random.key(seed), 5)
    return {
        "inputs": gaussian_with(key_of[0], (SEQS, L, D), 1.0, 6.0, ((0, 2), (1, 16)), (1, 2, 16, 2.0)),
        "filters": centred(key_of[1], (L, K), L ** -0.5, 0.09375, ((1, 8),), jnp.float32),
        "weights": centred(key_of[2], (K, D, DO), (K * D) ** -0.5, 0.03125, ((0, 8),)),
        "cotangent": centred(key_of[3], (SEQS, L, DO), ((L * SEQS) ** -0.5), 0.0625, ((0, 2), (1, 128))),
    }


def reference(inputs, filters, weights, cotangent):
    length = inputs.shape[1]
    filters_b = lax.optimization_barrier(filters.astype(jnp.bfloat16)).astype(jnp.float32)
    signal = jnp.fft.rfft(inputs.astype(jnp.float32), n=2 * length, axis=1)
    spectra = jnp.fft.rfft(filters_b, n=2 * length, axis=0)
    grad_rows = cotangent.reshape(SEQS, N_SEQ, CH, DO).astype(jnp.float32)

    def per_filter(running, filter_index):
        filter_spec = spectra[:, filter_index]
        features = jnp.fft.irfft(signal * filter_spec[None, :, None], n=2 * length, axis=1)[:, :length]
        features = features.astype(jnp.bfloat16)
        projected = jnp.dot(features.reshape(SEQS * length, D), weights[filter_index], preferred_element_type=jnp.float32)
        blocks = features.reshape(SEQS, N_SEQ, CH, D).astype(jnp.float32)
        partial_value = jnp.einsum("sbtd,sbto->sbdo", blocks, grad_rows, precision=lax.Precision.HIGHEST)
        partial_value = lax.optimization_barrier(partial_value.astype(jnp.bfloat16)).astype(jnp.float32)
        summed = jnp.sum(partial_value, axis=(0, 1)).astype(jnp.bfloat16)
        return running + projected.reshape(SEQS, length, DO), summed

    running, stacked = lax.scan(per_filter, jnp.zeros((SEQS, length, DO), jnp.float32), jnp.arange(K, dtype=jnp.int32))
    return running.astype(jnp.bfloat16), jnp.transpose(stacked, (1, 0, 2))
```

```python
import functools

import jax
import jax.numpy as jnp
from jax import lax
from jax.experimental import pallas as pl
from jax.experimental.pallas import tpu as pltpu
from jax.sharding import PartitionSpec as P

BF = jnp.bfloat16
F32 = jnp.float32
VMEM_LIMIT = 56 * 1024 * 1024


def params():
    return pltpu.CompilerParams(vmem_limit_bytes=VMEM_LIMIT)


def prep_kernel(n_chunk, x_ref, w_ref, y_ref):
    step = pl.program_id(0)
    per, rows, tokens = y_ref.shape
    width = x_ref.shape[1] // n_chunk
    count, _, cols = w_ref.shape
    sub = cols // per
    x = x_ref[...]
    for k in range(count):
        u = jnp.dot(x, w_ref[k], preferred_element_type=F32).T.astype(BF)
        for c in range(per):
            y_ref[c, width + k * sub : width + (k + 1) * sub, :] = u[c * sub : (c + 1) * sub]
    span = width * per
    xs = x_ref[:, pl.ds(pl.multiple_of(step * span, span), span)]
    xt = xs.T
    for c in range(per):
        y_ref[c, :width, :] = xt[c * width : (c + 1) * width]


def prep(x, w, n_chunk):
    tokens, width = x.shape
    count, _, out_width = w.shape
    steps = 4
    per = n_chunk // steps
    rows = width // n_chunk + count * (out_width // n_chunk)

    return pl.pallas_call(
        functools.partial(prep_kernel, n_chunk),
        grid=(steps,),
        out_shape=jax.ShapeDtypeStruct((n_chunk, rows, tokens), BF),
        in_specs=[
            pl.BlockSpec((tokens, width), lambda s: (0, 0)),
            pl.BlockSpec((count, width, out_width // steps), lambda s: (0, 0, s)),
        ],
        out_specs=pl.BlockSpec((per, rows, tokens), lambda s: (s, 0, 0)),
        compiler_params=params(),
    )(x, w)


def table_kernel(f_ref, z_ref):
    count, length, block = z_ref.shape
    n = length // block
    for k in range(count):
        for c in range(n):
            lag = block * (n - 1 - c)
            g = jnp.broadcast_to(f_ref[k : k + 1, lag : lag + 2 * block], (block, 2 * block))
            m = pltpu.roll(g, 0, 1, stride=1, stride_axis=0)[:, block:]
            z_ref[k, c * block : (c + 1) * block, :] = m.astype(BF)


def table(filters, block):
    length, count = filters.shape
    f = filters.T.astype(BF).astype(F32)
    f = jnp.pad(f, ((0, 0), (block, 0)))
    return pl.pallas_call(
        table_kernel,
        out_shape=jax.ShapeDtypeStruct((count, length, block), BF),
        compiler_params=params(),
    )(f)


def out_conv_kernel(parts, width, y_ref, z_ref, p_ref, u_ref):
    n, rows, block = y_ref.shape
    count = z_ref.shape[0]
    length = n * block
    sub = (rows - width) // count
    shifts = block // sub
    for k in range(count):
        for s in range(shifts):
            d = shifts - 1 - s
            if d:
                u_ref[k, s * sub : (s + 1) * sub, : d * block] = jnp.zeros((sub, d * block), BF)
            for j in range(n - d):
                u_ref[k, s * sub : (s + 1) * sub, (j + d) * block : (j + d + 1) * block] = y_ref[
                    j, width + k * sub : width + (k + 1) * sub, :
                ]
    piece = block // parts
    half = piece // 2
    for m in range(n // shifts):
        depth = (m + 1) * shifts * block
        acc = jnp.dot(u_ref[0, :, :depth], z_ref[0, length - depth :, :], preferred_element_type=F32)
        for k in range(1, count):
            acc += jnp.dot(u_ref[k, :, :depth], z_ref[k, length - depth :, :], preferred_element_type=F32)
        t = acc.T
        for s in range(shifts):
            i = m * shifts + s
            for j in range(parts):
                low = t[j * piece : j * piece + half, s * sub : (s + 1) * sub]
                high = t[j * piece + half : (j + 1) * piece, s * sub : (s + 1) * sub]
                p_ref[i * parts + j] = jnp.concatenate([low, high], axis=1).astype(BF)


def out_conv(y, z, parts, width):

    n, rows, block = y.shape
    count = z.shape[0]
    sub = (rows - width) // count
    return pl.pallas_call(
        functools.partial(out_conv_kernel, parts, width),
        out_shape=jax.ShapeDtypeStruct((n * parts, block // parts // 2, 2 * sub), BF),
        scratch_shapes=[pltpu.VMEM((count, block, n * block), BF)],
        compiler_params=params(),
    )(y, z)


def feature_kernel(width, y_ref, z_ref, f_ref, x_ref):
    n, rows, block = y_ref.shape
    count = z_ref.shape[0]
    length = n * block
    shifts = block // width
    for s in range(shifts):
        d = shifts - 1 - s
        if d:
            x_ref[s * width : (s + 1) * width, : d * block] = jnp.zeros((width, d * block), BF)
        for j in range(n - d):
            x_ref[s * width : (s + 1) * width, (j + d) * block : (j + d + 1) * block] = y_ref[j, :width, :]
    for m in range(n // shifts):
        depth = (m + 1) * shifts * block
        for k in range(count):
            acc = jnp.dot(x_ref[:, :depth], z_ref[k, length - depth :, :], preferred_element_type=F32).astype(BF)
            for s in range(shifts):
                i = m * shifts + s
                f_ref[k * width : (k + 1) * width, i * block : (i + 1) * block] = acc[s * width : (s + 1) * width]


def feature_conv(y, z, width):

    n, rows, block = y.shape
    count = z.shape[0]
    return pl.pallas_call(
        functools.partial(feature_kernel, width),
        out_shape=jax.ShapeDtypeStruct((count * width, n * block), BF),
        scratch_shapes=[pltpu.VMEM((block, n * block), BF)],
        compiler_params=params(),
    )(y, z)


def shards(n_seq, n_filt, inputs, filters, weights, cotangent):
    x = inputs[0]
    tokens, width = x.shape
    count, _, out_width = weights.shape
    own = width // n_seq
    sub = out_width // n_seq

    spread = jnp.broadcast_to(cotangent[0][None], (n_filt,) + cotangent.shape[1:])
    block_grad = lax.all_to_all(spread, "filt", 0, 0, tiled=True).reshape(tokens, out_width)
    full_grad = lax.all_gather(block_grad, "seq", axis=0, tiled=True)

    z = table(filters, tokens)
    y = prep(x, weights, n_seq)
    y = lax.all_to_all(y, "seq", 0, 0, tiled=True)

    p = out_conv(y, z, n_filt, own)
    p = lax.all_to_all(p, ("seq", "filt"), 0, 0, tiled=True)
    p = p.reshape(n_seq, n_filt, tokens // n_filt // 2, 2, sub).astype(F32).sum(axis=1)
    outputs = p.transpose(2, 1, 0, 3).reshape(1, tokens // n_filt, out_width).astype(BF)

    f = feature_conv(y, z, own)
    grad = jnp.dot(f, full_grad, preferred_element_type=F32).reshape(count, 2, own // 2, out_width)
    me = lax.axis_index("dp")
    mine = lax.dynamic_index_in_dim(grad, me, 1, keepdims=False)
    other = lax.dynamic_index_in_dim(grad, 1 - me, 1, keepdims=False)
    other = lax.ppermute(other, "dp", [(0, 1), (1, 0)])
    weight_grad = (mine + other).astype(BF).transpose(1, 0, 2)
    return outputs, weight_grad


def solution(mesh):

    in_specs = (
        P("dp", "seq", None),
        P(None, "filt"),
        P("filt", None, None),
        P("dp", ("seq", "filt"), None),
    )
    out_specs = (P("dp", ("seq", "filt"), None), P(("seq", "dp"), "filt", None))
    body = functools.partial(shards, mesh.shape["seq"], mesh.shape["filt"])
    return jax.shard_map(body, mesh=mesh, in_specs=in_specs, out_specs=out_specs, check_vma=False)
```

```python
import functools

import jax
import jax.numpy as jnp
from jax import lax
from jax.experimental import pallas as pl
from jax.experimental.pallas import tpu as pltpu
from jax.sharding import PartitionSpec as P

BF = jnp.bfloat16
F32 = jnp.float32
VMEM_LIMIT = 56 * 1024 * 1024
SIDE = 4


def params():
    return pltpu.CompilerParams(vmem_limit_bytes=VMEM_LIMIT)


def cost(flops, data):
    return pl.CostEstimate(flops=flops, bytes_accessed=data, transcendentals=0)


def turn_kernel(x_ref, y_ref):
    per, width, tokens = y_ref.shape
    xt = x_ref[...].T
    for c in range(per):
        y_ref[c] = xt[c * width : (c + 1) * width]


def turn(x, n_chunk):
    tokens, width = x.shape
    steps = 2
    own = width // n_chunk
    return pl.pallas_call(
        turn_kernel,
        grid=(steps,),
        out_shape=jax.ShapeDtypeStruct((n_chunk, own, tokens), BF),
        in_specs=[pl.BlockSpec((tokens, width // steps), lambda s: (0, s))],
        out_specs=pl.BlockSpec((n_chunk // steps, own, tokens), lambda s: (s, 0, 0)),
        compiler_params=params(),
        cost_estimate=cost(0, 4 * tokens * width),
    )(x)


def project_kernel(x_ref, w_ref, y_ref):
    per, rows, tokens = y_ref.shape
    count, _, cols = w_ref.shape
    sub = cols // per
    x = x_ref[...]
    for k in range(count):
        u = jnp.dot(x, w_ref[k], preferred_element_type=F32).T.astype(BF)
        for c in range(per):
            y_ref[c, k * sub : (k + 1) * sub, :] = u[c * sub : (c + 1) * sub]


def project(x, w, n_chunk):
    tokens, width = x.shape
    count, _, out_width = w.shape
    steps = 4
    rows = count * (out_width // n_chunk)
    return pl.pallas_call(
        project_kernel,
        grid=(steps,),
        out_shape=jax.ShapeDtypeStruct((n_chunk, rows, tokens), BF),
        in_specs=[
            pl.BlockSpec((tokens, width), lambda s: (0, 0)),
            pl.BlockSpec((count, width, out_width // steps), lambda s: (0, 0, s)),
        ],
        out_specs=pl.BlockSpec((n_chunk // steps, rows, tokens), lambda s: (s, 0, 0)),
        compiler_params=params(),
        cost_estimate=cost(2 * tokens * width * count * out_width, 2 * count * width * out_width),
    )(x, w)


def out_table_kernel(block, f_ref, z_ref):
    count, length, _ = z_ref.shape
    n = length // block
    for k in range(count):
        base = jnp.broadcast_to(f_ref[k : k + 1, :], (8, f_ref.shape[1]))
        base = pltpu.roll(base, 0, 1, stride=1, stride_axis=0)
        for g in range(block // 16):
            low = pltpu.roll(base, 16 * g, 1) if g else base
            high = pltpu.roll(base, 16 * g + 8, 1)
            rows = jnp.concatenate([low, high], axis=0).astype(BF)
            for c in range(n):
                z_ref[k, c * block + 16 * g : c * block + 16 * g + 16, :] = rows[:, (n - c) * block : (n - c + 1) * block]


def feature_table_kernel(block, f_ref, z_ref):
    length, cols = z_ref.shape
    count = f_ref.shape[0]
    half = cols // count
    n = length // block
    piece = 32
    lane = lax.broadcasted_iota(jnp.int32, (16, half), 1)
    first = lax.rem(lane, 2 * piece) < piece
    for k in range(count):
        base = jnp.broadcast_to(f_ref[k : k + 1, :], (8, f_ref.shape[1]))
        base = pltpu.roll(base, 0, 1, stride=1, stride_axis=0)
        rolled = {}

        def at(g):
            if g not in rolled:
                rolled[g] = pltpu.roll(base, 8 * g, 1) if g else base
            return rolled[g]

        for g in range(block // 16):
            a = jnp.concatenate([at(2 * g), at(2 * g + 1)], axis=0)
            b = jnp.concatenate([at(2 * g + 4), at(2 * g + 5)], axis=0)
            for c in range(n):
                start = (n - c) * block
                both = jnp.where(first, a[:, start : start + half], b[:, start + half : start + 2 * half])
                z_ref[c * block + 16 * g : c * block + 16 * g + 16, k * half : (k + 1) * half] = both.astype(BF)


def out_table(f, length, block):
    count = f.shape[0]
    return pl.pallas_call(
        functools.partial(out_table_kernel, block),
        out_shape=jax.ShapeDtypeStruct((count, length, block), BF),
        compiler_params=params(),
        cost_estimate=cost(0, 2 * count * length * block),
    )(f)


def feature_table(f, length, block):
    count = f.shape[0]
    return pl.pallas_call(
        functools.partial(feature_table_kernel, block),
        out_shape=jax.ShapeDtypeStruct((length, count * block // 2), BF),
        compiler_params=params(),
        cost_estimate=cost(0, count * length * block),
    )(f)


def out_conv_kernel(parts, y_ref, z_ref, p_ref, u_ref):
    n, rows, block = y_ref.shape
    count = z_ref.shape[0]
    sub = rows // count
    length = n * block
    shifts = block // sub
    for k in range(count):
        for s in range(shifts):
            d = shifts - 1 - s
            if d:
                u_ref[k, s * sub : (s + 1) * sub, : d * block] = jnp.zeros((sub, d * block), BF)
            for j in range(n - d):
                u_ref[k, s * sub : (s + 1) * sub, (j + d) * block : (j + d + 1) * block] = y_ref[
                    j, k * sub : (k + 1) * sub, :
                ]
    piece = block // parts
    half = piece // 2
    for m in range(n // shifts):
        depth = (m + 1) * shifts * block
        acc = jnp.dot(u_ref[0, :, :depth], z_ref[0, length - depth :, :], preferred_element_type=F32)
        for k in range(1, count):
            acc += jnp.dot(u_ref[k, :, :depth], z_ref[k, length - depth :, :], preferred_element_type=F32)
        t = acc.T
        for s in range(shifts):
            i = m * shifts + s
            for j in range(parts):
                low = t[j * piece : j * piece + half, s * sub : (s + 1) * sub]
                high = t[j * piece + half : (j + 1) * piece, s * sub : (s + 1) * sub]
                p_ref[i * parts + j] = jnp.concatenate([low, high], axis=1).astype(BF)


def out_conv(y, z, parts):
    n, rows, block = y.shape
    count = z.shape[0]
    sub = rows // count
    return pl.pallas_call(
        functools.partial(out_conv_kernel, parts),
        out_shape=jax.ShapeDtypeStruct((n * parts, block // parts // 2, 2 * sub), BF),
        scratch_shapes=[pltpu.VMEM((count, block, n * block), BF)],
        compiler_params=params(),
        cost_estimate=cost(2 * count * sub * (n * block) ** 2, 2 * count * n * block * block),
    )(y, z)


def feature_kernel(y_ref, z_ref, f_ref, x_ref):
    n, width, block = y_ref.shape
    length, cols = z_ref.shape
    half = block // 2
    count = cols // half
    shifts = block // width
    for s in range(shifts):
        d = shifts - 1 - s
        if d:
            x_ref[s * width : (s + 1) * width, : d * block] = jnp.zeros((width, d * block), BF)
        for j in range(n - d):
            x_ref[s * width : (s + 1) * width, (j + d) * block : (j + d + 1) * block] = y_ref[j]
    for m in range(n // shifts):
        depth = (m + 1) * shifts * block
        acc = jnp.dot(x_ref[:, :depth], z_ref[length - depth :, :], preferred_element_type=F32).astype(BF)
        for k in range(count):
            for s in range(shifts):
                i = m * shifts + s
                f_ref[k * width : (k + 1) * width, i * half : (i + 1) * half] = acc[
                    s * width : (s + 1) * width, k * half : (k + 1) * half
                ]


def feature_conv(y, z):
    n, width, block = y.shape
    length, cols = z.shape
    count = cols // (block // 2)
    return pl.pallas_call(
        feature_kernel,
        out_shape=jax.ShapeDtypeStruct((count * width, length // 2), BF),
        scratch_shapes=[pltpu.VMEM((block, length), BF)],
        compiler_params=params(),
        cost_estimate=cost(count * width * length * length, 2 * length * cols),
    )(y, z)


def grad_kernel(place_ref, f_ref, *refs):
    pieces, out_ref, grad_ref, sem = refs[:-3], refs[-3], refs[-2], refs[-1]
    half_rows = grad_ref.shape[0] // (SIDE * SIDE)
    half_cols = grad_ref.shape[1] // 2
    y, x = place_ref[0], place_ref[1]
    copies = []
    for side, group in enumerate((pieces[:5], pieces[5:])):
        for far in range(SIDE):
            for near in range(SIDE):
                if far == 0:
                    ref, index = group[0], near
                elif far == 1:
                    ref, index = group[1], near
                elif far == SIDE - 1:
                    ref, index = group[2], near
                elif near < SIDE // 2:
                    ref, index = group[3], near
                else:
                    ref, index = group[4], near - SIDE // 2
                dy, dx = (far, near) if side == 0 else (near, far)
                block = lax.rem(y + dy, SIDE) * SIDE + lax.rem(x + dx, SIDE)
                rows = pl.ds(pl.multiple_of(block * half_rows, half_rows), half_rows)
                copies.append(
                    pltpu.make_async_copy(
                        ref.at[index], grad_ref.at[rows, side * half_cols : (side + 1) * half_cols], sem.at[len(copies)]
                    )
                )
    for copy in copies:
        copy.start()
    for copy in copies:
        copy.wait()
    count = out_ref.shape[0]
    rows = f_ref.shape[0] // count
    for k in range(count):
        out_ref[k] = jnp.dot(f_ref[k * rows : (k + 1) * rows, :], grad_ref[...], preferred_element_type=F32).astype(BF)


def grad(f, pieces, place, count, out_width):
    rows, length = f.shape
    return pl.pallas_call(
        grad_kernel,
        out_shape=jax.ShapeDtypeStruct((count, rows // count, out_width), BF),
        in_specs=[pl.BlockSpec(memory_space=pltpu.SMEM), pl.BlockSpec(memory_space=pltpu.VMEM)]
        + [pl.BlockSpec(memory_space=pl.ANY)] * len(pieces),
        scratch_shapes=[pltpu.VMEM((length, out_width), BF), pltpu.SemaphoreType.DMA((2 * SIDE * SIDE,))],
        compiler_params=params(),
        cost_estimate=cost(2 * rows * length * out_width, 2 * length * out_width),
    )(place, f, *pieces)


def shift(axis, step):
    pairs = []
    for y in range(SIDE):
        for x in range(SIDE):
            to = ((y + step) % SIDE, x) if axis == "y" else (y, (x + step) % SIDE)
            pairs.append((y * SIDE + x, to[0] * SIDE + to[1]))
    return pairs


def move(a, axis, step):
    return lax.ppermute(a, "seq", shift(axis, step))


def plane_gather(a, near, far):
    ring = jnp.stack([a, move(a, near, -1), move(a, near, 2), move(a, near, 1)])
    after, before = move(ring, far, -1), move(ring, far, 1)
    h = SIDE // 2
    return [ring, after, before, move(before[:h], far, 1), move(after[h:], far, -1)]


def shards(n_seq, n_filt, inputs, filters, weights, cotangent):
    x = inputs[0]
    tokens, width = x.shape
    count, _, out_width = weights.shape
    length = filters.shape[0]
    sub = out_width // n_seq
    own = width // n_seq
    piece = tokens // n_filt
    at_seq, at_filt, at_dp = lax.axis_index("seq"), lax.axis_index("filt"), lax.axis_index("dp")
    parity = at_filt % 2

    c = cotangent[0]
    quads = [c] + [
        lax.ppermute(c, "filt", [((i + step) % n_filt, i) for i in range(n_filt)]) for step in (2, 4, 6)
    ]
    stack = jnp.stack(quads + quads)
    half = lax.dynamic_slice_in_dim(stack, (n_filt // 2 - at_filt // 2) % (n_filt // 2), n_filt // 2, 0)
    half = jnp.stack([half[0], half[2], half[1], half[3]]).reshape(tokens // 2, out_width)

    xs = lax.all_to_all(turn(x, n_seq), "seq", 0, 0, tiled=True)
    us = lax.all_to_all(project(x, weights, n_seq), "seq", 0, 0, tiled=True)

    pieces = plane_gather(half[:, : out_width // 2], "x", "y") + plane_gather(half[:, out_width // 2 :], "y", "x")

    fb = filters.T.astype(BF)
    other = lax.ppermute(fb, "filt", [(i, i ^ 1) for i in range(n_filt)])
    pad = ((0, 0), (tokens, tokens))
    pair = jnp.pad(jnp.concatenate([fb, other]).astype(F32), pad)
    pair = lax.dynamic_slice_in_dim(pair, piece * parity, length + tokens, 1)
    z_out = out_table(jnp.pad(fb.astype(F32), ((0, 0), (tokens, 0))), length, tokens)
    z_feature = feature_table(pair, length, tokens)

    f = feature_conv(xs, z_feature)
    p = out_conv(us, z_out, n_filt)
    p = lax.all_to_all(p, ("seq", "filt"), 0, 0, tiled=True)
    p = p.reshape(n_seq, n_filt, piece // 2, 2, sub).astype(F32).sum(axis=1)
    outputs = p.transpose(2, 1, 0, 3).reshape(1, piece, out_width).astype(BF)

    place = jnp.stack([at_seq // SIDE, at_seq % SIDE]).astype(jnp.int32)
    g = grad(f, pieces, place, 2 * count, out_width).reshape(2 * count, 2, own // 2, out_width)
    mine = lax.dynamic_index_in_dim(g, at_dp, 1, keepdims=False)
    rest = lax.dynamic_index_in_dim(g, 1 - at_dp, 1, keepdims=False)
    total = mine.astype(F32) + lax.ppermute(rest, "dp", [(0, 1), (1, 0)]).astype(F32)
    back = lax.ppermute(total[count:].astype(BF), "filt", [(i, i ^ 1) for i in range(n_filt)])
    weight_grad = (total[:count] + back.astype(F32)).astype(BF).transpose(1, 0, 2)
    return outputs, weight_grad


def solution(mesh):
    in_specs = (
        P("dp", "seq", None),
        P(None, "filt"),
        P("filt", None, None),
        P("dp", ("seq", "filt"), None),
    )
    out_specs = (P("dp", ("seq", "filt"), None), P(("seq", "dp"), "filt", None))
    body = functools.partial(shards, mesh.shape["seq"], mesh.shape["filt"])
    return jax.shard_map(body, mesh=mesh, in_specs=in_specs, out_specs=out_specs, check_vma=False)
```

```python
import functools

import jax
import jax.numpy as jnp
from jax import lax
from jax.experimental import pallas as pl
from jax.experimental.pallas import tpu as pltpu
from jax.sharding import PartitionSpec as P

BF = jnp.bfloat16
F32 = jnp.float32
VMEM_LIMIT = 16 * 1024 * 1024


def params():
    return pltpu.CompilerParams(vmem_limit_bytes=VMEM_LIMIT)


def cost(microseconds):
    return pl.CostEstimate(flops=0, bytes_accessed=int(microseconds * 3.6e6), transcendentals=0)


def turn_kernel(x_ref, y_ref):
    per, width, tokens = y_ref.shape
    xt = x_ref[...].T
    for c in range(per):
        y_ref[c] = xt[c * width : (c + 1) * width]


def turn(x, n_chunk):
    tokens, width = x.shape
    steps = 2
    own = width // n_chunk
    return pl.pallas_call(
        turn_kernel,
        grid=(steps,),
        out_shape=jax.ShapeDtypeStruct((n_chunk, own, tokens), BF),
        in_specs=[pl.BlockSpec((tokens, width // steps), lambda s: (0, s))],
        out_specs=pl.BlockSpec((n_chunk // steps, own, tokens), lambda s: (s, 0, 0)),
        compiler_params=params(),
        cost_estimate=cost(2.3),
    )(x)


def project_kernel(x_ref, w_ref, y_ref):
    per, rows, tokens = y_ref.shape
    count, _, cols = w_ref.shape
    sub = cols // per
    x = x_ref[...]
    for k in range(count):
        u = jnp.dot(x, w_ref[k], preferred_element_type=F32).astype(BF).T
        for c in range(per):
            y_ref[c, k * sub : (k + 1) * sub, :] = u[c * sub : (c + 1) * sub]


def project(x, w, n_chunk):
    tokens, width = x.shape
    count, _, out_width = w.shape
    steps = 4
    rows = count * (out_width // n_chunk)
    return pl.pallas_call(
        project_kernel,
        grid=(steps,),
        out_shape=jax.ShapeDtypeStruct((n_chunk, rows, tokens), BF),
        in_specs=[
            pl.BlockSpec((tokens, width), lambda s: (0, 0)),
            pl.BlockSpec((count, width, out_width // steps), lambda s: (0, 0, s)),
        ],
        out_specs=pl.BlockSpec((n_chunk // steps, rows, tokens), lambda s: (s, 0, 0)),
        compiler_params=params(),
        cost_estimate=cost(7),
    )(x, w)


def out_table_kernel(block, f_ref, z_ref):
    count, length, _ = z_ref.shape
    n = length // block
    for k in range(count):
        base = jnp.broadcast_to(f_ref[k : k + 1, :], (8, f_ref.shape[1]))
        base = pltpu.roll(base, 0, 1, stride=1, stride_axis=0)
        for g in range(block // 16):
            low = pltpu.roll(base, 16 * g, 1) if g else base
            high = pltpu.roll(base, 16 * g + 8, 1)
            rows = jnp.concatenate([low, high], axis=0).astype(BF)
            for c in range(n):
                z_ref[k, c * block + 16 * g : c * block + 16 * g + 16, :] = rows[:, (n - c) * block : (n - c + 1) * block]


def feature_table_kernel(block, f_ref, z_ref):
    length, cols = z_ref.shape
    count = f_ref.shape[0]
    half = cols // count
    n = length // block
    piece = 32
    lane = lax.broadcasted_iota(jnp.int32, (16, half), 1)
    first = lax.rem(lane, 2 * piece) < piece
    for k in range(count):
        base = jnp.broadcast_to(f_ref[k : k + 1, :], (8, f_ref.shape[1]))
        base = pltpu.roll(base, 0, 1, stride=1, stride_axis=0)
        rolled = {}

        def at(g):
            if g not in rolled:
                rolled[g] = pltpu.roll(base, 8 * g, 1) if g else base
            return rolled[g]

        for g in range(block // 16):
            a = jnp.concatenate([at(2 * g), at(2 * g + 1)], axis=0)
            b = jnp.concatenate([at(2 * g + 4), at(2 * g + 5)], axis=0)
            for c in range(n):
                start = (n - c) * block
                both = jnp.where(first, a[:, start : start + half], b[:, start + half : start + 2 * half])
                z_ref[c * block + 16 * g : c * block + 16 * g + 16, k * half : (k + 1) * half] = both.astype(BF)


def out_table(f, length, block):
    count = f.shape[0]
    return pl.pallas_call(
        functools.partial(out_table_kernel, block),
        out_shape=jax.ShapeDtypeStruct((count, length, block), BF),
        compiler_params=params(),
        cost_estimate=cost(3.6),
    )(f)


def feature_table(f, length, block):
    count = f.shape[0]
    return pl.pallas_call(
        functools.partial(feature_table_kernel, block),
        out_shape=jax.ShapeDtypeStruct((length, count * block // 2), BF),
        compiler_params=params(),
        cost_estimate=cost(5),
    )(f)


def out_conv_kernel(parts, y_ref, z_ref, p_ref, u_ref):
    n, rows, block = y_ref.shape
    count = z_ref.shape[0]
    sub = rows // count
    length = n * block
    shifts = block // sub
    for k in range(count):
        for s in range(shifts):
            d = shifts - 1 - s
            if d:
                u_ref[k, s * sub : (s + 1) * sub, : d * block] = jnp.zeros((sub, d * block), BF)
            for j in range(n - d):
                u_ref[k, s * sub : (s + 1) * sub, (j + d) * block : (j + d + 1) * block] = y_ref[
                    j, k * sub : (k + 1) * sub, :
                ]
    piece = block // parts
    half = piece // 2
    for m in range(n // shifts):
        depth = (m + 1) * shifts * block
        acc = jnp.dot(u_ref[0, :, :depth], z_ref[0, length - depth :, :], preferred_element_type=F32)
        for k in range(1, count):
            acc += jnp.dot(u_ref[k, :, :depth], z_ref[k, length - depth :, :], preferred_element_type=F32)
        t = acc.T
        for s in range(shifts):
            i = m * shifts + s
            for j in range(parts):
                low = t[j * piece : j * piece + half, s * sub : (s + 1) * sub]
                high = t[j * piece + half : (j + 1) * piece, s * sub : (s + 1) * sub]
                p_ref[i * parts + j] = jnp.concatenate([low, high], axis=1).astype(BF)


def out_conv(y, z, parts):
    n, rows, block = y.shape
    count = z.shape[0]
    sub = rows // count
    return pl.pallas_call(
        functools.partial(out_conv_kernel, parts),
        out_shape=jax.ShapeDtypeStruct((n * parts, block // parts // 2, 2 * sub), BF),
        scratch_shapes=[pltpu.VMEM((count, block, n * block), BF)],
        compiler_params=params(),
        cost_estimate=cost(6.5),
    )(y, z)


def feature_kernel(y_ref, z_ref, f_ref, x_ref):
    n, width, block = y_ref.shape
    length, cols = z_ref.shape
    half = block // 2
    count = cols // half
    shifts = block // width
    for s in range(shifts):
        d = shifts - 1 - s
        if d:
            x_ref[s * width : (s + 1) * width, : d * block] = jnp.zeros((width, d * block), BF)
        for j in range(n - d):
            x_ref[s * width : (s + 1) * width, (j + d) * block : (j + d + 1) * block] = y_ref[j]
    for m in range(n // shifts):
        depth = (m + 1) * shifts * block
        acc = jnp.dot(x_ref[:, :depth], z_ref[length - depth :, :], preferred_element_type=F32).astype(BF)
        for k in range(count):
            for s in range(shifts):
                i = m * shifts + s
                f_ref[k * width : (k + 1) * width, i * half : (i + 1) * half] = acc[
                    s * width : (s + 1) * width, k * half : (k + 1) * half
                ]


def feature_conv(y, z):
    n, width, block = y.shape
    length, cols = z.shape
    count = cols // (block // 2)
    return pl.pallas_call(
        feature_kernel,
        out_shape=jax.ShapeDtypeStruct((count * width, length // 2), BF),
        scratch_shapes=[pltpu.VMEM((block, length), BF)],
        compiler_params=params(),
        cost_estimate=cost(9),
    )(y, z)


def grad_kernel(steps, core_ref, f_hbm, g_hbm, rest_ref, mine_ref, f_ref, g_ref, acc_ref, sem):
    count, own, _ = mine_ref.shape
    rows, length = f_ref.shape
    depth = length // steps
    core = core_ref[0]
    copies = []
    for s in range(steps):
        at = pl.ds(s * depth, depth)
        copies.append(
            (
                pltpu.make_async_copy(f_hbm.at[:, at], f_ref.at[:, at], sem.at[2 * s]),
                pltpu.make_async_copy(g_hbm.at[at, :], g_ref.at[at, :], sem.at[2 * s + 1]),
            )
        )
    for group in copies:
        for copy in group:
            copy.start()
    for s in range(steps):
        for copy in copies[s]:
            copy.wait()
        at = slice(s * depth, (s + 1) * depth)
        part = jnp.dot(f_ref[:, at], g_ref[at, :], preferred_element_type=F32)
        if s:
            part += acc_ref[...]
        acc_ref[...] = part
    for k in range(count):
        for which, out_ref in ((1 - core, rest_ref), (core, mine_ref)):
            start = pl.multiple_of((2 * k + which) * own, own)
            out_ref[k] = acc_ref[pl.ds(start, own), :].astype(BF)


def grad(f, g, core, count):
    rows, length = f.shape
    cols = g.shape[1]
    steps = 4
    shape = jax.ShapeDtypeStruct((count, rows // count // 2, cols), BF)
    return pl.pallas_call(
        functools.partial(grad_kernel, steps),
        out_shape=(shape, shape),
        in_specs=[pl.BlockSpec(memory_space=pltpu.SMEM)] + [pl.BlockSpec(memory_space=pl.ANY)] * 2,
        scratch_shapes=[
            pltpu.VMEM((rows, length), BF),
            pltpu.VMEM((length, cols), BF),
            pltpu.VMEM((rows, cols), F32),
            pltpu.SemaphoreType.DMA((2 * steps,)),
        ],
        compiler_params=params(),
        cost_estimate=cost(5),
    )(core, f, g)


def finish_kernel(p_ref, o_ref):
    n, parts, half, lanes = p_ref.shape
    sub = lanes // 2
    for i in range(n // 2):
        pair = []
        for s in range(2):
            total = p_ref[2 * i + s, 0].astype(F32)
            for j in range(1, parts):
                total += p_ref[2 * i + s, j].astype(F32)
            pair.append(total)
        low = jnp.concatenate([pair[0][:, :sub], pair[1][:, :sub]], axis=1)
        high = jnp.concatenate([pair[0][:, sub:], pair[1][:, sub:]], axis=1)
        o_ref[:half, i * lanes : (i + 1) * lanes] = low.astype(BF)
        o_ref[half:, i * lanes : (i + 1) * lanes] = high.astype(BF)


def finish(p, n, parts):
    _, half, lanes = p.shape
    return pl.pallas_call(
        finish_kernel,
        out_shape=jax.ShapeDtypeStruct((2 * half, n * lanes // 2), BF),
        compiler_params=params(),
        cost_estimate=cost(1.8),
    )(p.reshape(n, parts, half, lanes))


def shards(n_seq, n_filt, inputs, filters, weights, cotangent):
    x = inputs[0]
    tokens, width = x.shape
    count, _, out_width = weights.shape
    length = filters.shape[0]
    sub = out_width // n_seq
    own = width // n_seq
    piece = tokens // n_filt
    at_filt, at_dp = lax.axis_index("filt"), lax.axis_index("dp")
    parity = at_filt % 2

    xt, c, fb = lax.optimization_barrier((turn(x, n_seq), cotangent[0], filters.T.astype(BF)))
    xs = lax.all_to_all(xt, "seq", 0, 0, tiled=True)

    quads = [c] + [
        lax.ppermute(c, "filt", [((i + step) % n_filt, i) for i in range(n_filt)]) for step in (2, 4, 6)
    ]
    half = lax.dynamic_slice_in_dim(jnp.stack(quads + quads), (n_filt // 2 - at_filt // 2) % (n_filt // 2), n_filt // 2, 0)
    half = jnp.stack([half[0], half[2], half[1], half[3]]).reshape(tokens // 2, out_width)
    full_grad = lax.all_gather(half, "seq", axis=0, tiled=True)

    other = lax.ppermute(fb, "filt", [(i, i ^ 1) for i in range(n_filt)])
    pad = ((0, 0), (tokens, tokens))
    pair = jnp.pad(jnp.concatenate([fb, other]).astype(F32), pad)
    pair = lax.dynamic_slice_in_dim(pair, piece * parity, length + tokens, 1)
    z_out = out_table(jnp.pad(fb.astype(F32), ((0, 0), (tokens, 0))), length, tokens)
    z_feature = feature_table(pair, length, tokens)

    u = project(x, weights, n_seq)
    xs, u, z_out, z_feature = lax.optimization_barrier((xs, u, z_out, z_feature))
    us = lax.all_to_all(u, "seq", 0, 0, tiled=True)
    f = feature_conv(xs, z_feature)

    us, z_out, f = lax.optimization_barrier((us, z_out, f))
    p, f = lax.optimization_barrier((out_conv(us, z_out, n_filt), f))
    p = lax.all_to_all(p, ("seq", "filt"), 0, 0, tiled=True)

    rest, mine = grad(f, full_grad, at_dp.astype(jnp.int32)[None], 2 * count)
    total = mine.astype(F32) + lax.ppermute(rest, "dp", [(0, 1), (1, 0)]).astype(F32)
    send, p = lax.optimization_barrier((total[count:].astype(BF), p))
    back = lax.ppermute(send, "filt", [(i, i ^ 1) for i in range(n_filt)])
    weight_grad = (total[:count] + back.astype(F32)).astype(BF).transpose(1, 0, 2)
    outputs = finish(p, n_seq, n_filt)[None]
    return outputs, weight_grad


def solution(mesh):
    in_specs = (
        P("dp", "seq", None),
        P(None, "filt"),
        P("filt", None, None),
        P("dp", ("seq", "filt"), None),
    )
    out_specs = (P("dp", ("seq", "filt"), None), P(("seq", "dp"), "filt", None))
    body = functools.partial(shards, mesh.shape["seq"], mesh.shape["filt"])
    return jax.shard_map(body, mesh=mesh, in_specs=in_specs, out_specs=out_specs, check_vma=False)
```

```python
import functools

import jax
import jax.numpy as jnp
from jax import lax
from jax.experimental import pallas as pl
from jax.experimental.pallas import tpu as pltpu
from jax.sharding import PartitionSpec as P

BF = jnp.bfloat16
F32 = jnp.float32
VMEM_LIMIT = 16 * 1024 * 1024
GRAD_LIMIT = 57 * 1024 * 1024


DONE = jax.ShapeDtypeStruct((8, 128), F32)


def params(limit=None):
    return pltpu.CompilerParams(vmem_limit_bytes=limit or VMEM_LIMIT)


def cost(microseconds):
    return pl.CostEstimate(flops=0, bytes_accessed=int(microseconds * 3.6e6), transcendentals=0)


def turn_kernel(x_ref, y_ref):
    per, width, tokens = y_ref.shape
    xt = x_ref[...].T
    for c in range(per):
        y_ref[c] = xt[c * width : (c + 1) * width]


def turn(x, n_chunk):
    tokens, width = x.shape
    steps = 2
    own = width // n_chunk
    return pl.pallas_call(
        turn_kernel,
        grid=(steps,),
        out_shape=jax.ShapeDtypeStruct((n_chunk, own, tokens), BF),
        in_specs=[pl.BlockSpec((tokens, width // steps), lambda s: (0, s))],
        out_specs=pl.BlockSpec((n_chunk // steps, own, tokens), lambda s: (s, 0, 0)),
        compiler_params=params(),
        cost_estimate=cost(1.3),
    )(x)


def project_kernel(x_ref, w_ref, y_ref):
    per, rows, tokens = y_ref.shape
    count, _, cols = w_ref.shape
    sub = cols // per
    x = x_ref[...]
    for k in range(count):
        u = jnp.dot(x, w_ref[k], preferred_element_type=F32).astype(BF).T
        for c in range(per):
            y_ref[c, k * sub : (k + 1) * sub, :] = u[c * sub : (c + 1) * sub]


def project(x, w, n_chunk):
    tokens, width = x.shape
    count, _, out_width = w.shape
    steps = 4
    rows = count * (out_width // n_chunk)
    return pl.pallas_call(
        project_kernel,
        grid=(steps,),
        out_shape=jax.ShapeDtypeStruct((n_chunk, rows, tokens), BF),
        in_specs=[
            pl.BlockSpec((tokens, width), lambda s: (0, 0)),
            pl.BlockSpec((count, width, out_width // steps), lambda s: (0, 0, s)),
        ],
        out_specs=pl.BlockSpec((n_chunk // steps, rows, tokens), lambda s: (s, 0, 0)),
        compiler_params=params(),
        cost_estimate=cost(0.01),
    )(x, w)


def fill_out_table(block, f_ref, z_ref):
    count, length, _ = z_ref.shape
    n = length // block
    for k in range(count):
        base = jnp.broadcast_to(f_ref[k : k + 1, :], (8, f_ref.shape[1]))
        base = pltpu.roll(base, 0, 1, stride=1, stride_axis=0)
        for g in range(block // 16):
            low = pltpu.roll(base, 16 * g, 1) if g else base
            high = pltpu.roll(base, 16 * g + 8, 1)
            rows = jnp.concatenate([low, high], axis=0).astype(BF)
            for c in range(n):
                z_ref[k, c * block + 16 * g : c * block + 16 * g + 16, :] = rows[:, (n - c) * block : (n - c + 1) * block]


def feature_table_kernel(block, f_ref, z_ref, done_ref):
    done_ref[...] = jnp.zeros_like(done_ref)
    length, cols = z_ref.shape
    count = f_ref.shape[0]
    half = cols // count
    n = length // block
    piece = 32
    lane = lax.broadcasted_iota(jnp.int32, (16, half), 1)
    first = lax.rem(lane, 2 * piece) < piece
    for k in range(count):
        base = jnp.broadcast_to(f_ref[k : k + 1, :], (8, f_ref.shape[1]))
        base = pltpu.roll(base, 0, 1, stride=1, stride_axis=0)
        rolled = {}

        def at(g):
            if g not in rolled:
                rolled[g] = pltpu.roll(base, 8 * g, 1) if g else base
            return rolled[g]

        for g in range(block // 16):
            a = jnp.concatenate([at(2 * g), at(2 * g + 1)], axis=0)
            b = jnp.concatenate([at(2 * g + 4), at(2 * g + 5)], axis=0)
            for c in range(n):
                start = (n - c) * block
                both = jnp.where(first, a[:, start : start + half], b[:, start + half : start + 2 * half])
                z_ref[c * block + 16 * g : c * block + 16 * g + 16, k * half : (k + 1) * half] = both.astype(BF)


def feature_table(f, length, block):
    count = f.shape[0]
    return pl.pallas_call(
        functools.partial(feature_table_kernel, block),
        out_shape=(jax.ShapeDtypeStruct((length, count * block // 2), BF), DONE),
        compiler_params=params(),
        cost_estimate=cost(0.01),
    )(f)


def out_conv_kernel(parts, y_ref, f_ref, *refs):
    p_ref, done_ref, u_ref, z_ref = refs[-4:]
    fill_out_table(y_ref.shape[2], f_ref, z_ref)
    done_ref[...] = jnp.zeros_like(done_ref)
    n, rows, block = y_ref.shape
    count = z_ref.shape[0]
    sub = rows // count
    length = n * block
    shifts = block // sub
    for k in range(count):
        for s in range(shifts):
            d = shifts - 1 - s
            if d:
                u_ref[k, s * sub : (s + 1) * sub, : d * block] = jnp.zeros((sub, d * block), BF)
            for j in range(n - d):
                u_ref[k, s * sub : (s + 1) * sub, (j + d) * block : (j + d + 1) * block] = y_ref[
                    j, k * sub : (k + 1) * sub, :
                ]
    piece = block // parts
    half = piece // 2
    for m in range(n // shifts):
        depth = (m + 1) * shifts * block
        acc = jnp.dot(u_ref[0, :, :depth], z_ref[0, length - depth :, :], preferred_element_type=F32)
        for k in range(1, count):
            acc += jnp.dot(u_ref[k, :, :depth], z_ref[k, length - depth :, :], preferred_element_type=F32)
        t = acc.T
        for s in range(shifts):
            i = m * shifts + s
            for j in range(parts):
                low = t[j * piece : j * piece + half, s * sub : (s + 1) * sub]
                high = t[j * piece + half : (j + 1) * piece, s * sub : (s + 1) * sub]
                p_ref[i * parts + j] = jnp.concatenate([low, high], axis=1).astype(BF)


def out_conv(y, f, parts, after):
    n, rows, block = y.shape
    count = f.shape[0]
    sub = rows // count
    return pl.pallas_call(
        functools.partial(out_conv_kernel, parts),
        out_shape=(jax.ShapeDtypeStruct((n * parts, block // parts // 2, 2 * sub), BF), DONE),
        in_specs=[pl.BlockSpec(memory_space=pltpu.VMEM)] * 2 + [pl.BlockSpec(memory_space=pl.ANY)] * len(after),
        scratch_shapes=[pltpu.VMEM((count, block, n * block), BF), pltpu.VMEM((count, n * block, block), BF)],
        compiler_params=params(),
        cost_estimate=cost(5.0),
    )(y, f, *after)


def feature_kernel(y_ref, z_ref, f_ref, done_ref, x_ref):
    done_ref[...] = jnp.zeros_like(done_ref)
    n, width, block = y_ref.shape
    length, cols = z_ref.shape
    half = block // 2
    count = cols // half
    shifts = block // width
    for s in range(shifts):
        d = shifts - 1 - s
        if d:
            x_ref[s * width : (s + 1) * width, : d * block] = jnp.zeros((width, d * block), BF)
        for j in range(n - d):
            x_ref[s * width : (s + 1) * width, (j + d) * block : (j + d + 1) * block] = y_ref[j]
    for m in range(n // shifts):
        depth = (m + 1) * shifts * block
        acc = jnp.dot(x_ref[:, :depth], z_ref[length - depth :, :], preferred_element_type=F32).astype(BF)
        for k in range(count):
            for s in range(shifts):
                i = m * shifts + s
                f_ref[k * width : (k + 1) * width, i * half : (i + 1) * half] = acc[
                    s * width : (s + 1) * width, k * half : (k + 1) * half
                ]


def feature_conv(y, z):
    n, width, block = y.shape
    length, cols = z.shape
    count = cols // (block // 2)
    return pl.pallas_call(
        feature_kernel,
        out_shape=(jax.ShapeDtypeStruct((count * width, length // 2), BF), DONE),
        scratch_shapes=[pltpu.VMEM((block, length), BF)],
        compiler_params=params(),
        cost_estimate=cost(5.0),
    )(y, z)


def grad_kernel(steps, place_ref, f_hbm, g_hbm, _, rest_ref, mine_ref, f_ref, g_ref, acc_ref, sem):
    count, own, _ = mine_ref.shape
    rows, length = f_ref.shape
    blocks, quarters, piece, width = g_ref.shape
    depth = length // steps
    per = blocks // steps
    core, first = place_ref[0], place_ref[1]
    copies = []
    for s in range(steps):
        at = pl.ds(s * per, per)
        group = [pltpu.make_async_copy(f_hbm.at[:, pl.ds(s * depth, depth)], f_ref.at[:, pl.ds(s * depth, depth)], sem.at[s, quarters])]
        for r in range(quarters):
            quarter = lax.rem(first + r, quarters)
            to = lax.rem(quarter, 2) * 2 + quarter // 2
            group.append(pltpu.make_async_copy(g_hbm.at[at, r], g_ref.at[at, to], sem.at[s, r]))
        copies.append(group)
    for copy in copies[0] + copies[1]:
        copy.start()
    for s in range(steps):
        for copy in copies[s]:
            copy.wait()
        if s + 2 < steps:
            for copy in copies[s + 2]:
                copy.start()
        at = slice(s * depth, (s + 1) * depth)
        g = g_ref[s * per : (s + 1) * per].reshape(depth, width)
        part = jnp.dot(f_ref[:, at], g, preferred_element_type=F32)
        acc_ref[...] = part if s == 0 else acc_ref[...] + part
    for k in range(count):
        low, high = acc_ref[2 * k * own : (2 * k + 1) * own], acc_ref[(2 * k + 1) * own : (2 * k + 2) * own]
        mine_ref[k] = jnp.where(core == 0, low, high).astype(BF)
        rest_ref[k] = jnp.where(core == 0, high, low).astype(BF)


def grad(f, g, place, count, after):
    rows, length = f.shape
    width = g.shape[-1]
    steps = 4
    shape = jax.ShapeDtypeStruct((count, rows // count // 2, width), BF)
    return pl.pallas_call(
        functools.partial(grad_kernel, steps),
        out_shape=(shape, shape),
        in_specs=[pl.BlockSpec(memory_space=pltpu.SMEM)] + [pl.BlockSpec(memory_space=pl.ANY)] * 3,
        scratch_shapes=[
            pltpu.VMEM((rows, length), BF),
            pltpu.VMEM(g.shape, BF),
            pltpu.VMEM((rows, width), F32),
            pltpu.SemaphoreType.DMA((steps, g.shape[1] + 1)),
        ],
        compiler_params=params(GRAD_LIMIT),
        cost_estimate=cost(5.0),
    )(place, f, g, after)


def finish_kernel(p_ref, o_ref):
    n, parts, half, lanes = p_ref.shape
    sub = lanes // 2
    for i in range(n // 2):
        pair = []
        for s in range(2):
            total = p_ref[2 * i + s, 0].astype(F32)
            for j in range(1, parts):
                total += p_ref[2 * i + s, j].astype(F32)
            pair.append(total)
        low = jnp.concatenate([pair[0][:, :sub], pair[1][:, :sub]], axis=1)
        high = jnp.concatenate([pair[0][:, sub:], pair[1][:, sub:]], axis=1)
        o_ref[:half, i * lanes : (i + 1) * lanes] = low.astype(BF)
        o_ref[half:, i * lanes : (i + 1) * lanes] = high.astype(BF)


def finish(p, n, parts):
    _, half, lanes = p.shape
    return pl.pallas_call(
        finish_kernel,
        out_shape=jax.ShapeDtypeStruct((2 * half, n * lanes // 2), BF),
        compiler_params=params(),
        cost_estimate=cost(0.8),
    )(p.reshape(n, parts, half, lanes))


def shards(n_seq, n_filt, inputs, filters, weights, cotangent):
    x = inputs[0]
    tokens, width = x.shape
    count, _, out_width = weights.shape
    length = filters.shape[0]
    sub = out_width // n_seq
    own = width // n_seq
    piece = tokens // n_filt
    at_filt, at_dp = lax.axis_index("filt"), lax.axis_index("dp")
    parity = at_filt % 2

    quads = [cotangent[0]] + [
        lax.ppermute(cotangent[0], "filt", [((i + step) % n_filt, i) for i in range(n_filt)]) for step in (2, 4, 6)
    ]

    fb = filters.T.astype(BF)
    xt, quads = lax.optimization_barrier((turn(x, n_seq), quads))
    full_grad = lax.all_gather(jnp.concatenate(quads), "seq", axis=0, tiled=True)
    full_grad = full_grad.reshape(n_seq, n_filt // 2, piece, out_width)
    xs = lax.all_to_all(xt, "seq", 0, 0, tiled=True)

    other = lax.ppermute(fb, "filt", [(i, i ^ 1) for i in range(n_filt)])
    pad = ((0, 0), (tokens, tokens))
    pair = jnp.pad(jnp.concatenate([fb, other]).astype(F32), pad)
    pair = lax.dynamic_slice_in_dim(pair, piece * parity, length + tokens, 1)
    alone = jnp.pad(fb.astype(F32), ((0, 0), (tokens, 0)))
    z_feature, done_feature = feature_table(pair, length, tokens)

    u = project(x, weights, n_seq)
    xs, u, *after = lax.optimization_barrier((xs, u, done_feature))
    us = lax.all_to_all(u, "seq", 0, 0, tiled=True)
    f, done_f = feature_conv(xs, z_feature)

    us, *late = lax.optimization_barrier((us, done_f))
    p, done_p = out_conv(us, alone, n_filt, after + late)
    place = jnp.stack([at_dp, at_filt // 2]).astype(jnp.int32)
    p = lax.all_to_all(p, ("seq", "filt"), 0, 0, tiled=True)

    rest, mine = grad(f, full_grad, place, 2 * count, done_p)
    total = mine.astype(F32) + lax.ppermute(rest, "dp", [(0, 1), (1, 0)]).astype(F32)
    send, p = lax.optimization_barrier((total[count:].astype(BF), p))
    back = lax.ppermute(send, "filt", [(i, i ^ 1) for i in range(n_filt)])
    weight_grad = (total[:count] + back.astype(F32)).astype(BF).transpose(1, 0, 2)
    outputs = finish(p, n_seq, n_filt)[None]
    return outputs, weight_grad


def solution(mesh):
    in_specs = (
        P("dp", "seq", None),
        P(None, "filt"),
        P("filt", None, None),
        P("dp", ("seq", "filt"), None),
    )
    out_specs = (P("dp", ("seq", "filt"), None), P(("seq", "dp"), "filt", None))
    body = functools.partial(shards, mesh.shape["seq"], mesh.shape["filt"])
    return jax.shard_map(body, mesh=mesh, in_specs=in_specs, out_specs=out_specs, check_vma=False)
```

```python
import functools

import jax
import jax.numpy as jnp
from jax import lax
from jax.experimental import pallas as pl
from jax.experimental.pallas import tpu as pltpu
from jax.sharding import PartitionSpec as P

BF = jnp.bfloat16
F32 = jnp.float32
VMEM_LIMIT = 16 * 1024 * 1024
WIDE_LIMIT = 56 * 1024 * 1024
SIDE = 4


DONE = jax.ShapeDtypeStruct((8, 128), F32)


def params(limit=None):
    return pltpu.CompilerParams(vmem_limit_bytes=limit or VMEM_LIMIT)


def cost(microseconds):
    return pl.CostEstimate(flops=0, bytes_accessed=int(microseconds * 3.6e6), transcendentals=0)


def turn_kernel(x_ref, y_ref):
    per, width, tokens = y_ref.shape
    xt = x_ref[...].T
    for c in range(per):
        y_ref[c] = xt[c * width : (c + 1) * width]


def turn(x, n_chunk):
    tokens, width = x.shape
    steps = 2
    own = width // n_chunk
    return pl.pallas_call(
        turn_kernel,
        grid=(steps,),
        out_shape=jax.ShapeDtypeStruct((n_chunk, own, tokens), BF),
        in_specs=[pl.BlockSpec((tokens, width // steps), lambda s: (0, s))],
        out_specs=pl.BlockSpec((n_chunk // steps, own, tokens), lambda s: (s, 0, 0)),
        compiler_params=params(),
        cost_estimate=cost(1.3),
    )(x)


def project_kernel(x_ref, w_ref, y_ref):
    per, rows, tokens = y_ref.shape
    count, _, cols = w_ref.shape
    sub = cols // per
    x = x_ref[...]
    for k in range(count):
        u = jnp.dot(x, w_ref[k], preferred_element_type=F32).astype(BF).T
        for c in range(per):
            y_ref[c, k * sub : (k + 1) * sub, :] = u[c * sub : (c + 1) * sub]


def project(x, w, n_chunk):
    tokens, width = x.shape
    count, _, out_width = w.shape
    steps = 4
    rows = count * (out_width // n_chunk)
    return pl.pallas_call(
        project_kernel,
        grid=(steps,),
        out_shape=jax.ShapeDtypeStruct((n_chunk, rows, tokens), BF),
        in_specs=[
            pl.BlockSpec((tokens, width), lambda s: (0, 0)),
            pl.BlockSpec((count, width, out_width // steps), lambda s: (0, 0, s)),
        ],
        out_specs=pl.BlockSpec((n_chunk // steps, rows, tokens), lambda s: (s, 0, 0)),
        compiler_params=params(WIDE_LIMIT),
        cost_estimate=cost(7),
    )(x, w)


def fill_out_table(block, f_ref, z_ref):
    count, length, _ = z_ref.shape
    n = length // block
    for k in range(count):
        base = jnp.broadcast_to(f_ref[k : k + 1, :], (8, f_ref.shape[1]))
        base = pltpu.roll(base, 0, 1, stride=1, stride_axis=0)
        for g in range(block // 16):
            low = pltpu.roll(base, 16 * g, 1) if g else base
            high = pltpu.roll(base, 16 * g + 8, 1)
            rows = jnp.concatenate([low, high], axis=0).astype(BF)
            for c in range(n):
                z_ref[k, c * block + 16 * g : c * block + 16 * g + 16, :] = rows[:, (n - c) * block : (n - c + 1) * block]


def fill_feature_table(block, f_ref, z_ref):
    length, cols = z_ref.shape
    count = f_ref.shape[0]
    half = cols // count
    n = length // block
    piece = 32
    lane = lax.broadcasted_iota(jnp.int32, (16, half), 1)
    first = lax.rem(lane, 2 * piece) < piece
    for k in range(count):
        base = jnp.broadcast_to(f_ref[k : k + 1, :], (8, f_ref.shape[1]))
        base = pltpu.roll(base, 0, 1, stride=1, stride_axis=0)
        rolled = {}

        def at(g):
            if g not in rolled:
                rolled[g] = pltpu.roll(base, 8 * g, 1) if g else base
            return rolled[g]

        for g in range(block // 16):
            a = jnp.concatenate([at(2 * g), at(2 * g + 1)], axis=0)
            b = jnp.concatenate([at(2 * g + 4), at(2 * g + 5)], axis=0)
            for c in range(n):
                start = (n - c) * block
                both = jnp.where(first, a[:, start : start + half], b[:, start + half : start + 2 * half])
                z_ref[c * block + 16 * g : c * block + 16 * g + 16, k * half : (k + 1) * half] = both.astype(BF)


def out_conv_kernel(parts, y_ref, f_ref, *refs):
    p_ref, done_ref, u_ref, z_ref = refs[-4:]
    fill_out_table(y_ref.shape[2], f_ref, z_ref)
    done_ref[...] = jnp.zeros_like(done_ref)
    n, rows, block = y_ref.shape
    count = z_ref.shape[0]
    sub = rows // count
    length = n * block
    shifts = block // sub
    for k in range(count):
        for s in range(shifts):
            d = shifts - 1 - s
            if d:
                u_ref[k, s * sub : (s + 1) * sub, : d * block] = jnp.zeros((sub, d * block), BF)
            for j in range(n - d):
                u_ref[k, s * sub : (s + 1) * sub, (j + d) * block : (j + d + 1) * block] = y_ref[
                    j, k * sub : (k + 1) * sub, :
                ]
    piece = block // parts
    half = piece // 2
    for m in range(n // shifts):
        depth = (m + 1) * shifts * block
        acc = jnp.dot(u_ref[0, :, :depth], z_ref[0, length - depth :, :], preferred_element_type=F32)
        for k in range(1, count):
            acc += jnp.dot(u_ref[k, :, :depth], z_ref[k, length - depth :, :], preferred_element_type=F32)
        t = acc.T
        for s in range(shifts):
            i = m * shifts + s
            for j in range(parts):
                low = t[j * piece : j * piece + half, s * sub : (s + 1) * sub]
                high = t[j * piece + half : (j + 1) * piece, s * sub : (s + 1) * sub]
                p_ref[i * parts + j] = jnp.concatenate([low, high], axis=1).astype(BF)


def out_conv(y, f, parts, after):
    n, rows, block = y.shape
    count = f.shape[0]
    sub = rows // count
    return pl.pallas_call(
        functools.partial(out_conv_kernel, parts),
        out_shape=(jax.ShapeDtypeStruct((n * parts, block // parts // 2, 2 * sub), BF), DONE),
        in_specs=[pl.BlockSpec(memory_space=pltpu.VMEM)] * 2 + [pl.BlockSpec(memory_space=pl.ANY)] * len(after),
        scratch_shapes=[pltpu.VMEM((count, block, n * block), BF), pltpu.VMEM((count, n * block, block), BF)],
        compiler_params=params(),
        cost_estimate=cost(5.0),
    )(y, f, *after)


def feature_kernel(y_ref, taps_ref, f_ref, done_ref, x_ref, z_ref):
    done_ref[...] = jnp.zeros_like(done_ref)
    n, width, block = y_ref.shape
    fill_feature_table(block, taps_ref, z_ref)
    length, cols = z_ref.shape
    half = block // 2
    count = cols // half
    shifts = block // width
    for s in range(shifts):
        d = shifts - 1 - s
        if d:
            x_ref[s * width : (s + 1) * width, : d * block] = jnp.zeros((width, d * block), BF)
        for j in range(n - d):
            x_ref[s * width : (s + 1) * width, (j + d) * block : (j + d + 1) * block] = y_ref[j]
    for m in range(n // shifts):
        depth = (m + 1) * shifts * block
        acc = jnp.dot(x_ref[:, :depth], z_ref[length - depth :, :], preferred_element_type=F32).astype(BF)
        for k in range(count):
            for s in range(shifts):
                i = m * shifts + s
                f_ref[k * width : (k + 1) * width, i * half : (i + 1) * half] = acc[
                    s * width : (s + 1) * width, k * half : (k + 1) * half
                ]


def feature_conv(y, taps):
    n, width, block = y.shape
    length = n * block
    count = taps.shape[0]
    return pl.pallas_call(
        feature_kernel,
        out_shape=(jax.ShapeDtypeStruct((count * width, length // 2), BF), DONE),
        scratch_shapes=[pltpu.VMEM((block, length), BF), pltpu.VMEM((length, count * block // 2), BF)],
        compiler_params=params(),
        cost_estimate=cost(5.0),
    )(y, taps)


def grad_kernel(place_ref, f_ref, *refs):
    pieces, (rest_ref, mine_ref, grad_ref, sem) = refs[: 2 * SIDE], refs[-4:]
    count, own, _ = mine_ref.shape
    half_rows = grad_ref.shape[1] // (SIDE * SIDE)
    cols = grad_ref.shape[2]
    y, x, core = place_ref[0], place_ref[1], place_ref[2]
    copies = []
    for side in range(2):
        for far in range(SIDE):
            for near in range(SIDE):
                dy, dx = (far, near) if side == 0 else (near, far)
                block = lax.rem(y + SIDE - dy, SIDE) * SIDE + lax.rem(x + SIDE - dx, SIDE)
                rows = pl.ds(pl.multiple_of(block * half_rows, half_rows), half_rows)
                copies.append(
                    pltpu.make_async_copy(
                        pieces[side * SIDE + far].at[near], grad_ref.at[side, rows, :], sem.at[len(copies)]
                    )
                )
    for copy in copies:
        copy.start()
    for side in range(2):
        for copy in copies[side * SIDE * SIDE : (side + 1) * SIDE * SIDE]:
            copy.wait()
        part = jnp.dot(f_ref[...], grad_ref[side], preferred_element_type=F32).astype(BF)
        at = slice(side * cols, (side + 1) * cols)
        for k in range(count):
            low, high = part[2 * k * own : (2 * k + 1) * own], part[(2 * k + 1) * own : (2 * k + 2) * own]
            mine_ref[k, :, at] = jnp.where(core == 0, low, high)
            rest_ref[k, :, at] = jnp.where(core == 0, high, low)


def grad(f, pieces, place, count, out_width, after):
    rows, length = f.shape
    shape = jax.ShapeDtypeStruct((count, rows // count // 2, out_width), BF)
    return pl.pallas_call(
        grad_kernel,
        out_shape=(shape, shape),
        in_specs=[pl.BlockSpec(memory_space=pltpu.SMEM), pl.BlockSpec(memory_space=pltpu.VMEM)]
        + [pl.BlockSpec(memory_space=pl.ANY)] * (len(pieces) + 1),
        scratch_shapes=[
            pltpu.VMEM((2, length, out_width // 2), BF),
            pltpu.SemaphoreType.DMA((2 * SIDE * SIDE,)),
        ],
        compiler_params=params(),
        cost_estimate=cost(5),
    )(place, f, *pieces, after)


def shift(axis, step):
    pairs = []
    for y in range(SIDE):
        for x in range(SIDE):
            to = ((y + step) % SIDE, x) if axis == "y" else (y, (x + step) % SIDE)
            pairs.append((y * SIDE + x, to[0] * SIDE + to[1]))
    return pairs


def step(a, axis, d):
    return lax.ppermute(a, "seq", shift(axis, d))


def ring(a, axis):
    return [a] + [step(a, axis, d) for d in range(1, SIDE)]


def finish_kernel(p_ref, o_ref):
    n, parts, half, lanes = p_ref.shape
    sub = lanes // 2
    for i in range(n // 2):
        pair = []
        for s in range(2):
            total = p_ref[2 * i + s, 0].astype(F32)
            for j in range(1, parts):
                total += p_ref[2 * i + s, j].astype(F32)
            pair.append(total)
        low = jnp.concatenate([pair[0][:, :sub], pair[1][:, :sub]], axis=1)
        high = jnp.concatenate([pair[0][:, sub:], pair[1][:, sub:]], axis=1)
        o_ref[:half, i * lanes : (i + 1) * lanes] = low.astype(BF)
        o_ref[half:, i * lanes : (i + 1) * lanes] = high.astype(BF)


def finish(p, n, parts):
    _, half, lanes = p.shape
    return pl.pallas_call(
        finish_kernel,
        out_shape=jax.ShapeDtypeStruct((2 * half, n * lanes // 2), BF),
        compiler_params=params(),
        cost_estimate=cost(0.8),
    )(p.reshape(n, parts, half, lanes))


def shards(n_seq, n_filt, inputs, filters, weights, cotangent):
    x = inputs[0]
    tokens, width = x.shape
    count, _, out_width = weights.shape
    length = filters.shape[0]
    sub = out_width // n_seq
    own = width // n_seq
    piece = tokens // n_filt
    at_seq, at_filt, at_dp = lax.axis_index("seq"), lax.axis_index("filt"), lax.axis_index("dp")
    parity = at_filt % 2

    quads = [cotangent[0]] + [
        lax.ppermute(cotangent[0], "filt", [((i + step) % n_filt, i) for i in range(n_filt)]) for step in (2, 4, 6)
    ]

    fb = filters.T.astype(BF)
    xs = lax.all_to_all(turn(x, n_seq), "seq", 0, 0, tiled=True)
    other = lax.ppermute(fb, "filt", [(i, i ^ 1) for i in range(n_filt)])
    u, quads, other = lax.optimization_barrier((project(x, weights, n_seq), quads, other))
    half = lax.dynamic_slice_in_dim(jnp.stack(quads + quads), (n_filt // 2 - at_filt // 2) % (n_filt // 2), n_filt // 2, 0)
    half = jnp.stack([half[0], half[2], half[1], half[3]]).reshape(tokens // 2, out_width)
    left = ring(half[:, : out_width // 2], "x")
    half = half[:, out_width // 2 :]
    right = [half, step(half, "y", 1), step(half, "y", 3)]

    pad = ((0, 0), (tokens, tokens))
    pair = jnp.pad(jnp.concatenate([fb, other]).astype(F32), pad)
    pair = lax.dynamic_slice_in_dim(pair, piece * parity, length + tokens, 1)
    alone = jnp.pad(fb.astype(F32), ((0, 0), (tokens, 0)))

    xs, u = lax.optimization_barrier((xs, u))
    us = lax.all_to_all(u, "seq", 0, 0, tiled=True)
    f, done_f = feature_conv(xs, pair)

    left, half, done_f = lax.optimization_barrier((left, half, done_f))
    left = jnp.stack(left)
    pieces = [left] + [step(left, "y", d) for d in range(1, SIDE)]
    right.insert(2, step(half, "y", 2))

    p, done_p = out_conv(us, alone, n_filt, [done_f])
    right, done_p = lax.optimization_barrier((right, done_p))
    right = jnp.stack(right)
    pieces += [right] + [step(right, "x", d) for d in range(1, SIDE)]
    p = lax.all_to_all(p, ("seq", "filt"), 0, 0, tiled=True)

    place = jnp.stack([at_seq // SIDE, at_seq % SIDE, at_dp]).astype(jnp.int32)
    rest, mine = grad(f, pieces, place, 2 * count, out_width, done_p)
    total = mine.astype(F32) + lax.ppermute(rest, "dp", [(0, 1), (1, 0)]).astype(F32)
    send, p = lax.optimization_barrier((total[count:].astype(BF), p))
    back = lax.ppermute(send, "filt", [(i, i ^ 1) for i in range(n_filt)])
    weight_grad = (total[:count] + back.astype(F32)).astype(BF).transpose(1, 0, 2)
    outputs = finish(p, n_seq, n_filt)[None]
    return outputs, weight_grad


def solution(mesh):
    in_specs = (
        P("dp", "seq", None),
        P(None, "filt"),
        P("filt", None, None),
        P("dp", ("seq", "filt"), None),
    )
    out_specs = (P("dp", ("seq", "filt"), None), P(("seq", "dp"), "filt", None))
    body = functools.partial(shards, mesh.shape["seq"], mesh.shape["filt"])
    return jax.shard_map(body, mesh=mesh, in_specs=in_specs, out_specs=out_specs, check_vma=False)
```

```python
import functools

import jax
import jax.numpy as jnp
from jax import lax
from jax.experimental import pallas as pl
from jax.experimental.pallas import tpu as pltpu
from jax.sharding import PartitionSpec as P

BF = jnp.bfloat16
F32 = jnp.float32
VMEM_LIMIT = 16 * 1024 * 1024
WIDE_LIMIT = 56 * 1024 * 1024
SIDE = 4


DONE = jax.ShapeDtypeStruct((8, 128), F32)


def params(limit=None):
    return pltpu.CompilerParams(vmem_limit_bytes=limit or VMEM_LIMIT)


def cost(microseconds):
    return pl.CostEstimate(flops=0, bytes_accessed=int(microseconds * 3.6e6), transcendentals=0)


def turn_kernel(x_ref, y_ref):
    per, width, tokens = y_ref.shape
    xt = x_ref[...].T
    for c in range(per):
        y_ref[c] = xt[c * width : (c + 1) * width]


def turn(x, n_chunk):
    tokens, width = x.shape
    steps = 2
    own = width // n_chunk
    return pl.pallas_call(
        turn_kernel,
        grid=(steps,),
        out_shape=jax.ShapeDtypeStruct((n_chunk, own, tokens), BF),
        in_specs=[pl.BlockSpec((tokens, width // steps), lambda s: (0, s))],
        out_specs=pl.BlockSpec((n_chunk // steps, own, tokens), lambda s: (s, 0, 0)),
        compiler_params=params(),
        cost_estimate=cost(1.3),
    )(x)


def project_kernel(x_ref, w_ref, y_ref):
    per, rows, tokens = y_ref.shape
    count, _, cols = w_ref.shape
    sub = cols // per
    x = x_ref[...]
    for k in range(count):
        u = jnp.dot(x, w_ref[k], preferred_element_type=F32).astype(BF).T
        for c in range(per):
            y_ref[c, k * sub : (k + 1) * sub, :] = u[c * sub : (c + 1) * sub]


def project(x, w, n_chunk):
    tokens, width = x.shape
    count, _, out_width = w.shape
    steps = 4
    rows = count * (out_width // n_chunk)
    return pl.pallas_call(
        project_kernel,
        grid=(steps,),
        out_shape=jax.ShapeDtypeStruct((n_chunk, rows, tokens), BF),
        in_specs=[
            pl.BlockSpec((tokens, width), lambda s: (0, 0)),
            pl.BlockSpec((count, width, out_width // steps), lambda s: (0, 0, s)),
        ],
        out_specs=pl.BlockSpec((n_chunk // steps, rows, tokens), lambda s: (s, 0, 0)),
        compiler_params=params(WIDE_LIMIT),
        cost_estimate=cost(7),
    )(x, w)


def fill_out_table(block, f_ref, z_ref):
    count, length, _ = z_ref.shape
    n = length // block
    for k in range(count):
        base = jnp.broadcast_to(f_ref[k : k + 1, :], (8, f_ref.shape[1]))
        base = pltpu.roll(base, 0, 1, stride=1, stride_axis=0)
        for g in range(block // 16):
            low = pltpu.roll(base, 16 * g, 1) if g else base
            high = pltpu.roll(base, 16 * g + 8, 1)
            rows = jnp.concatenate([low, high], axis=0).astype(BF)
            for c in range(n):
                z_ref[k, c * block + 16 * g : c * block + 16 * g + 16, :] = rows[:, (n - c) * block : (n - c + 1) * block]


def fill_feature_table(block, f_ref, z_ref):
    length, cols = z_ref.shape
    count = f_ref.shape[0]
    half = cols // count
    n = length // block
    piece = 32
    lane = lax.broadcasted_iota(jnp.int32, (16, half), 1)
    first = lax.rem(lane, 2 * piece) < piece
    for k in range(count):
        base = jnp.broadcast_to(f_ref[k : k + 1, :], (8, f_ref.shape[1]))
        base = pltpu.roll(base, 0, 1, stride=1, stride_axis=0)
        rolled = {}

        def at(g):
            if g not in rolled:
                rolled[g] = pltpu.roll(base, 8 * g, 1) if g else base
            return rolled[g]

        for g in range(block // 16):
            a = jnp.concatenate([at(2 * g), at(2 * g + 1)], axis=0)
            b = jnp.concatenate([at(2 * g + 4), at(2 * g + 5)], axis=0)
            for c in range(n):
                start = (n - c) * block
                both = jnp.where(first, a[:, start : start + half], b[:, start + half : start + 2 * half])
                z_ref[c * block + 16 * g : c * block + 16 * g + 16, k * half : (k + 1) * half] = both.astype(BF)


def out_conv_kernel(parts, y_ref, f_ref, *refs):
    p_ref, done_ref, u_ref, z_ref = refs[-4:]
    fill_out_table(y_ref.shape[2], f_ref, z_ref)
    done_ref[...] = jnp.zeros_like(done_ref)
    n, rows, block = y_ref.shape
    count = z_ref.shape[0]
    sub = rows // count
    length = n * block
    shifts = block // sub
    for k in range(count):
        for s in range(shifts):
            d = shifts - 1 - s
            if d:
                u_ref[k, s * sub : (s + 1) * sub, : d * block] = jnp.zeros((sub, d * block), BF)
            for j in range(n - d):
                u_ref[k, s * sub : (s + 1) * sub, (j + d) * block : (j + d + 1) * block] = y_ref[
                    j, k * sub : (k + 1) * sub, :
                ]
    piece = block // parts
    half = piece // 2
    for m in range(n // shifts):
        depth = (m + 1) * shifts * block
        acc = jnp.dot(u_ref[0, :, :depth], z_ref[0, length - depth :, :], preferred_element_type=F32)
        for k in range(1, count):
            acc += jnp.dot(u_ref[k, :, :depth], z_ref[k, length - depth :, :], preferred_element_type=F32)
        t = acc.T
        for s in range(shifts):
            i = m * shifts + s
            for j in range(parts):
                low = t[j * piece : j * piece + half, s * sub : (s + 1) * sub]
                high = t[j * piece + half : (j + 1) * piece, s * sub : (s + 1) * sub]
                p_ref[i * parts + j] = jnp.concatenate([low, high], axis=1).astype(BF)


def out_conv(y, f, parts, after):
    n, rows, block = y.shape
    count = f.shape[0]
    sub = rows // count
    return pl.pallas_call(
        functools.partial(out_conv_kernel, parts),
        out_shape=(jax.ShapeDtypeStruct((n * parts, block // parts // 2, 2 * sub), BF), DONE),
        in_specs=[pl.BlockSpec(memory_space=pltpu.VMEM)] * 2 + [pl.BlockSpec(memory_space=pl.ANY)] * len(after),
        scratch_shapes=[pltpu.VMEM((count, block, n * block), BF), pltpu.VMEM((count, n * block, block), BF)],
        compiler_params=params(),
        cost_estimate=cost(5.0),
    )(y, f, *after)


def feature_kernel(y_ref, taps_ref, f_ref, done_ref, x_ref, z_ref):
    done_ref[...] = jnp.zeros_like(done_ref)
    n, width, block = y_ref.shape
    fill_feature_table(block, taps_ref, z_ref)
    length, cols = z_ref.shape
    half = block // 2
    count = cols // half
    shifts = block // width
    for s in range(shifts):
        d = shifts - 1 - s
        if d:
            x_ref[s * width : (s + 1) * width, : d * block] = jnp.zeros((width, d * block), BF)
        for j in range(n - d):
            x_ref[s * width : (s + 1) * width, (j + d) * block : (j + d + 1) * block] = y_ref[j]
    for m in range(n // shifts):
        depth = (m + 1) * shifts * block
        acc = jnp.dot(x_ref[:, :depth], z_ref[length - depth :, :], preferred_element_type=F32).astype(BF)
        for k in range(count):
            for s in range(shifts):
                i = m * shifts + s
                f_ref[k * width : (k + 1) * width, i * half : (i + 1) * half] = acc[
                    s * width : (s + 1) * width, k * half : (k + 1) * half
                ]


def feature_conv(y, taps):
    n, width, block = y.shape
    length = n * block
    count = taps.shape[0]
    return pl.pallas_call(
        feature_kernel,
        out_shape=(jax.ShapeDtypeStruct((count * width, length // 2), BF), DONE),
        scratch_shapes=[pltpu.VMEM((block, length), BF), pltpu.VMEM((length, count * block // 2), BF)],
        compiler_params=params(),
        cost_estimate=cost(5.0),
    )(y, taps)


def grad_kernel(place_ref, f_ref, *refs):
    pieces, (rest_ref, mine_ref, grad_ref, sem) = refs[: 2 * SIDE], refs[-4:]
    count, own, _ = mine_ref.shape
    half_rows = grad_ref.shape[1] // (SIDE * SIDE)
    cols = grad_ref.shape[2]
    y, x, core = place_ref[0], place_ref[1], place_ref[2]
    copies = []
    for side in range(2):
        for far in range(SIDE):
            for near in range(SIDE):
                dy, dx = (far, near) if side == 0 else (near, far)
                block = lax.rem(y + SIDE - dy, SIDE) * SIDE + lax.rem(x + SIDE - dx, SIDE)
                rows = pl.ds(pl.multiple_of(block * half_rows, half_rows), half_rows)
                copies.append(
                    pltpu.make_async_copy(
                        pieces[side * SIDE + far].at[near], grad_ref.at[side, rows, :], sem.at[len(copies)]
                    )
                )
    for copy in copies[: SIDE * SIDE]:
        copy.start()
    for side in range(2):
        for copy in copies[side * SIDE * SIDE : (side + 1) * SIDE * SIDE]:
            copy.wait()
        if side == 0:
            for copy in copies[SIDE * SIDE :]:
                copy.start()
        part = jnp.dot(f_ref[...], grad_ref[side], preferred_element_type=F32).astype(BF)
        at = slice(side * cols, (side + 1) * cols)
        for k in range(count):
            low, high = part[2 * k * own : (2 * k + 1) * own], part[(2 * k + 1) * own : (2 * k + 2) * own]
            mine_ref[k, :, at] = jnp.where(core == 0, low, high)
            rest_ref[k, :, at] = jnp.where(core == 0, high, low)


def grad(f, pieces, place, count, out_width, after):
    rows, length = f.shape
    shape = jax.ShapeDtypeStruct((count, rows // count // 2, out_width), BF)
    return pl.pallas_call(
        grad_kernel,
        out_shape=(shape, shape),
        in_specs=[pl.BlockSpec(memory_space=pltpu.SMEM), pl.BlockSpec(memory_space=pltpu.VMEM)]
        + [pl.BlockSpec(memory_space=pl.ANY)] * (len(pieces) + 1),
        scratch_shapes=[
            pltpu.VMEM((2, length, out_width // 2), BF),
            pltpu.SemaphoreType.DMA((2 * SIDE * SIDE,)),
        ],
        compiler_params=params(),
        cost_estimate=cost(5),
    )(place, f, *pieces, after)


def shift(axis, step):
    pairs = []
    for y in range(SIDE):
        for x in range(SIDE):
            to = ((y + step) % SIDE, x) if axis == "y" else (y, (x + step) % SIDE)
            pairs.append((y * SIDE + x, to[0] * SIDE + to[1]))
    return pairs


def step(a, axis, d):
    return lax.ppermute(a, "seq", shift(axis, d))


def ring(a, axis):
    return [a] + [step(a, axis, d) for d in range(1, SIDE)]


def finish_kernel(p_ref, o_ref):
    n, parts, half, lanes = p_ref.shape
    sub = lanes // 2
    for i in range(n // 2):
        pair = []
        for s in range(2):
            total = p_ref[2 * i + s, 0].astype(F32)
            for j in range(1, parts):
                total += p_ref[2 * i + s, j].astype(F32)
            pair.append(total)
        low = jnp.concatenate([pair[0][:, :sub], pair[1][:, :sub]], axis=1)
        high = jnp.concatenate([pair[0][:, sub:], pair[1][:, sub:]], axis=1)
        o_ref[:half, i * lanes : (i + 1) * lanes] = low.astype(BF)
        o_ref[half:, i * lanes : (i + 1) * lanes] = high.astype(BF)


def finish(p, n, parts):
    _, half, lanes = p.shape
    return pl.pallas_call(
        finish_kernel,
        out_shape=jax.ShapeDtypeStruct((2 * half, n * lanes // 2), BF),
        compiler_params=params(),
        cost_estimate=cost(0.8),
    )(p.reshape(n, parts, half, lanes))


def shards(n_seq, n_filt, inputs, filters, weights, cotangent):
    x = inputs[0]
    tokens, width = x.shape
    count, _, out_width = weights.shape
    length = filters.shape[0]
    sub = out_width // n_seq
    own = width // n_seq
    piece = tokens // n_filt
    at_seq, at_filt, at_dp = lax.axis_index("seq"), lax.axis_index("filt"), lax.axis_index("dp")
    parity = at_filt % 2

    quads = [cotangent[0]] + [
        lax.ppermute(cotangent[0], "filt", [((i + step) % n_filt, i) for i in range(n_filt)]) for step in (2, 4, 6)
    ]

    fb = filters.T.astype(BF)
    xs = lax.all_to_all(turn(x, n_seq), "seq", 0, 0, tiled=True)
    other = lax.ppermute(fb, "filt", [(i, i ^ 1) for i in range(n_filt)])
    u, quads, other = lax.optimization_barrier((project(x, weights, n_seq), quads, other))
    half = lax.dynamic_slice_in_dim(jnp.stack(quads + quads), (n_filt // 2 - at_filt // 2) % (n_filt // 2), n_filt // 2, 0)
    half = jnp.stack([half[0], half[2], half[1], half[3]]).reshape(tokens // 2, out_width)
    left = ring(half[:, : out_width // 2], "x")
    half = half[:, out_width // 2 :]
    right = [half, step(half, "y", 1), step(half, "y", 3)]

    pad = ((0, 0), (tokens, tokens))
    pair = jnp.pad(jnp.concatenate([fb, other]).astype(F32), pad)
    pair = lax.dynamic_slice_in_dim(pair, piece * parity, length + tokens, 1)
    alone = jnp.pad(fb.astype(F32), ((0, 0), (tokens, 0)))

    xs, u = lax.optimization_barrier((xs, u))
    us = lax.all_to_all(u, "seq", 0, 0, tiled=True)
    f, done_f = feature_conv(xs, pair)

    left, half, done_f = lax.optimization_barrier((left, half, done_f))
    left = jnp.stack(left)
    pieces = [left] + [step(left, "y", d) for d in range(1, SIDE)]
    right.insert(2, step(half, "y", 2))

    p, done_p = out_conv(us, alone, n_filt, [done_f])
    right, done_p = lax.optimization_barrier((right, done_p))
    right = jnp.stack(right)
    pieces += [right] + [step(right, "x", d) for d in range(1, SIDE)]
    p = lax.all_to_all(p, ("seq", "filt"), 0, 0, tiled=True)

    place = jnp.stack([at_seq // SIDE, at_seq % SIDE, at_dp]).astype(jnp.int32)
    rest, mine = grad(f, pieces, place, 2 * count, out_width, done_p)
    total = mine.astype(F32) + lax.ppermute(rest, "dp", [(0, 1), (1, 0)]).astype(F32)
    send, p = lax.optimization_barrier((total[count:].astype(BF), p))
    back = lax.ppermute(send, "filt", [(i, i ^ 1) for i in range(n_filt)])
    weight_grad = (total[:count] + back.astype(F32)).astype(BF).transpose(1, 0, 2)
    outputs = finish(p, n_seq, n_filt)[None]
    return outputs, weight_grad


def solution(mesh):
    in_specs = (
        P("dp", "seq", None),
        P(None, "filt"),
        P("filt", None, None),
        P("dp", ("seq", "filt"), None),
    )
    out_specs = (P("dp", ("seq", "filt"), None), P(("seq", "dp"), "filt", None))
    body = functools.partial(shards, mesh.shape["seq"], mesh.shape["filt"])
    return jax.shard_map(body, mesh=mesh, in_specs=in_specs, out_specs=out_specs, check_vma=False)
```
